32 devices in a mesh: tm: 8 (over z, x), space: 4 (over y, core).
Axes of the slice: x: 2, y: 2, z: 4, core: 2. Of those that a mesh axis runs over, the one named last changes fastest.
Arguments:
- source: float32 [64, 8, 128, 128], P('tm', 'space'), may hold values from -6 to 6
- thrust_axial: float32 [8, 128, 128], P('space'), may hold values from -6 to 6
- thrust_lateral: float32 [8, 128, 128], P('space'), may hold values from -6 to 6
- yaw_index: int32 [16], P('tm'), may hold values from 0 to 23
- diffusivity: float32 [8, 128, 128], P('space'), may hold values from 0.5 to 1
- cotangent: float32 [64, 8, 128, 128], P('tm', 'space'), may hold values from -6 to 6
Outputs:
- forward_state: float32 [64, 8, 128, 128], P('tm', 'space')
- adjoint_state: float32 [64, 8, 128, 128], P('tm', 'space')
The draws below stay inside these ranges and needn't reach their ends.
All inputs are finite; a program needn't handle non-finite values.
Results may differ from the reference program's by a relative error of at most 0.00002.
Values sent between devices are 32-bit elements; how exact they have to be, the bound alone decides.
A program may use at most 64 MiB of HBM per device.

```python
import math
import jax
import jax.numpy as jnp
from jax import lax

NY = 128
NX = 128
YAWS = 24
NT = 64
BLOCKS = 16
NZ = 8


def with_ends(values, stream_key, smallest, largest):
    longest = values.shape.index(max(values.shape))
    spots = []
    for shift in (0, 1):
        where = [jax.random.randint(jax.random.fold_in(stream_key, axis), (), 0, length) for axis, length in enumerate(values.shape)]
        where[longest] = (where[longest] + shift) % values.shape[longest]
        spots.append(tuple(where))
    return values.at[spots[0]].set(smallest).at[spots[1]].set(largest)


def block_scale(stream_key, dims, split, smallest, top_value):
    loudness, own = 1.0, jax.random.fold_in(stream_key, 6)
    for position, blocks in split:
        heights = jnp.exp(jax.random.uniform(jax.random.fold_in(own, position), (blocks,), jnp.float32, smallest / len(split), top_value / len(split)))
        loudness = loudness * jnp.repeat(heights, dims[position] // blocks).reshape([-1 if axis == position else 1 for axis in range(len(dims))])
    return loudness


def noise(own_key, extent, deviation, bound, pieces=(), dtype=jnp.bfloat16):
    entries = jax.random.normal(own_key, extent, jnp.float32) * deviation
    if len(pieces) > 0:
        entries = block_scale(own_key, extent, pieces, -0.22, 0.18) * entries
    return jnp.clip(entries, min=-bound, max=bound).astype(dtype)


def setup_inputs(seed: int = 0) -> dict:
    keys = jax.random.split(jax.random.key(seed), 7)
    return {
        "source": noise(keys[0], (NT, NZ, NY, NX), 1.0, 6.0, ((0, 8), (1, 4)), jnp.float32),
        "thrust_axial": noise(keys[1], (NZ, NY, NX), 1.0, 6.0, ((0, 4),), jnp.float32),
        "thrust_lateral": noise(keys[2], (NZ, NY, NX), 1.0, 6.0, ((0, 4),), jnp.float32),
        "yaw_index": with_ends(jax.random.randint(keys[3], (BLOCKS,), 0, YAWS), jax.random.fold_in(keys[3], 1), 0, YAWS - 1).astype(jnp.int32),
        "diffusivity": jnp.clip(jnp.exp(math.log(1.0) - 0.6931472 * jax.random.uniform(keys[4], (NZ, NY, NX), jnp.float32) ** block_scale(keys[4], (NZ, NY, NX), ((0, 4),), -0.2, 0.2)), 0.5, 1.0),
        "cotangent": noise(keys[5], (NT, NZ, NY, NX), 1.0, 6.0, ((0, 8), (1, 4)), jnp.float32),
    }


tau_levels = (0.03, 0.06, 0.08)
drift_x = 0.3
drift_y = 0.2


def second_diff(padded):
    centre = padded[:, 1:-1]
    neighbours = padded[:, 2:] + padded[:, :-2]
    neighbours = neighbours + jnp.roll(centre, 1, 2) + jnp.roll(centre, -1, 2)
    neighbours = neighbours + jnp.roll(centre, 1, 3) + jnp.roll(centre, -1, 3)
    return neighbours - 6.0 * centre


def with_faces(field):
    return jnp.pad(field, ((0, 0), (1, 1), (0, 0), (0, 0)))


def drift(field):
    along_x = jnp.roll(field, -1, 3) - jnp.roll(field, 1, 3)
    along_y = jnp.roll(field, -1, 2) - jnp.roll(field, 1, 2)
    return 0.5 * drift_x * along_x + 0.5 * drift_y * along_y


def forward_step(field, diffusivity, depth_level):
    step_size = tau_levels[depth_level]
    curvature = second_diff(with_faces(field))
    return field + step_size * (diffusivity * curvature) - step_size * drift(field)


def adjoint_step(field, diffusivity, depth_level):
    step_size = tau_levels[depth_level]
    curvature = second_diff(with_faces(diffusivity * field))
    return field + step_size * curvature + step_size * drift(field)


def cycle(rhs_blocks, advance):
    marched = rhs_blocks[:, 0]
    marched = advance(marched, 0) + rhs_blocks[:, 1]
    marched = advance(marched, 0) + rhs_blocks[:, 2]
    residual = advance(marched, 0) + rhs_blocks[:, 3]
    groups = residual.reshape((residual.shape[0] // 4, 4) + residual.shape[1:])
    middle = advance(groups[:, 0], 1) + groups[:, 1]
    middle = advance(middle, 1) + groups[:, 2]
    coarse_rhs = advance(middle, 1) + groups[:, 3]

    def coarse_turn(carried, piece):
        updated = advance(carried[None], 2)[0] + piece
        return updated, updated

    final_value, solved = lax.scan(coarse_turn, jnp.zeros_like(coarse_rhs[0]), coarse_rhs)
    earlier = jnp.concatenate([jnp.zeros_like(solved[:1]), solved[:-1]], 0)
    leading = advance(earlier, 1) + groups[:, 0]
    second = advance(leading, 1) + groups[:, 1]
    trailing = advance(second, 1) + groups[:, 2]
    level_one = jnp.stack([leading, second, trailing, solved], 1).reshape(residual.shape)
    before = jnp.concatenate([jnp.zeros_like(level_one[:1]), level_one[:-1]], 0)
    fine_first = advance(before, 0) + rhs_blocks[:, 0]
    fine_second = advance(fine_first, 0) + rhs_blocks[:, 1]
    fine_third = advance(fine_second, 0) + rhs_blocks[:, 2]
    points = jnp.stack([fine_first, fine_second, fine_third, level_one], 1)
    return points.reshape((-1,) + residual.shape[1:])


def reference(source, thrust_axial, thrust_lateral, yaw_index, diffusivity, cotangent):
    blocks = yaw_index.shape[0]
    angle = (2.0 * math.pi / YAWS) * yaw_index.astype(jnp.float32)
    push = jnp.cos(angle)[:, None, None, None] * thrust_axial + jnp.sin(angle)[:, None, None, None] * thrust_lateral
    grid = source.shape[1:]
    forward_rhs = source.reshape((blocks, 4) + grid) + push[:, None]
    adjoint_rhs = cotangent[::-1].reshape((blocks, 4) + grid)

    def forward_advance(field, depth_level):
        return forward_step(field, diffusivity, depth_level)

    def adjoint_advance(field, depth_level):
        return adjoint_step(field, diffusivity, depth_level)

    forward_state = cycle(forward_rhs, forward_advance)
    adjoint_state = cycle(adjoint_rhs, adjoint_advance)[::-1]
    return forward_state, adjoint_state
```

```python
import functools
import math

import jax
import jax.numpy as jnp
from jax import lax
from jax.experimental import pallas as pl
from jax.experimental.pallas import tpu as pltpu
from jax.sharding import PartitionSpec as P

YAWS = 24
MESH = pl.DeviceIdType.MESH

tau_levels = (0.03, 0.06, 0.08)
drift_x = 0.3
drift_y = 0.2

HEAD, TAIL = 0, 1
H_R1, T_M1, T_M2 = 12, 13, 14
T_E, T_A1, T_A2, T_A3 = 15, 16, 17, 18
H_E, H_A1 = 19, 20
FINE = 21
EXCHANGES = 29
M1, R1, R2, E_TAIL, E_HEAD = 0, 1, 2, 3, 4


def fine_id(role, block, step):
    return (role * 2 + block) * 3 + step


def late_id(role, block, step):
    return FINE + (role * 2 + block) * 2 + step


def kernel(
    members, slabs,
    yaw, axial, lateral, kappa, source, cotangent,
    forward_out, adjoint_out,
    rhs, points, sent, below, above, own, push, march, resid, stage, passed,
    send_sem, recv_sem, pass_send, pass_recv, in_sem, out_sem,
):
    planes = kappa.shape[0]
    steps = source.shape[0]
    groups = members // 2
    tm, sp = lax.axis_index("tm"), lax.axis_index("space")
    dir_h = lax.rem(tm, 2)
    dir_t = 1 - dir_h
    sign_h = 1 - 2 * dir_h
    sign_t = -sign_h
    pos_h = jnp.where(dir_h == 0, tm, members - 1 - tm)
    g_h = pos_h // 2
    g_t = groups - 1 - g_h
    dirs = (dir_h, dir_t)
    lower, upper = sp > 0, sp < slabs - 1
    first_t, last_t = g_t == 0, g_t == groups - 1
    first_h = g_h == 0

    neighbours = (
        (lower, tm, sp - 1),
        (upper, tm, sp + 1),
        (tm > 0, tm - 1, sp),
        (tm < members - 1, tm + 1, sp),
        (jnp.logical_not(last_t), tm + 2 * sign_t, sp),
        (jnp.logical_not(first_t), tm - 2 * sign_t, sp),
    )
    barrier = pltpu.get_barrier_semaphore()
    count = 0
    for there, t, s in neighbours:
        count = count + there.astype(jnp.int32)

        @pl.when(there)
        def _():
            pl.semaphore_signal(barrier, inc=1, device_id=(t, s), device_id_type=MESH)

    def fetch(direction, j):
        if direction == 0:
            src = source.at[j]
        else:
            src = cotangent.at[steps - 1 - j]
        return pltpu.make_async_copy(src, rhs.at[direction, j], in_sem.at[direction, j])

    for i in range(4):
        for b in range(2):
            fetch(0, 4 * b + i).start()
            fetch(1, 4 * b + i).start()

    ones = jnp.ones(kappa.shape, jnp.float32)
    own[0, 0] = kappa[...]
    own[0, 1] = ones
    own[1, 0] = ones
    own[1, 1] = kappa[...]
    for b in range(2):
        angle = (2.0 * math.pi / YAWS) * jnp.full(kappa.shape[1:], yaw[b], jnp.int32).astype(jnp.float32)
        c, s = jnp.cos(angle[:8]), jnp.sin(angle[:8])
        reps = kappa.shape[1] // 8
        c, s = jnp.concatenate([c] * reps, 0), jnp.concatenate([s] * reps, 0)
        for z in range(planes):
            push[b, z] = c * axial[z] + s * lateral[z]

    nothing = jnp.zeros(below.shape[1:], jnp.float32)

    @pl.when(jnp.logical_not(lower))
    def _():
        def clear(e, carry):
            below[e] = nothing
            return carry
        lax.fori_loop(0, EXCHANGES, clear, 0)

    @pl.when(jnp.logical_not(upper))
    def _():
        def clear(e, carry):
            above[e] = nothing
            return carry
        lax.fori_loop(0, EXCHANGES, clear, 0)

    @pl.when(first_t)
    def _():
        for z in range(planes):
            passed[E_TAIL, z] = nothing

    @pl.when(first_h)
    def _():
        for z in range(planes):
            passed[E_HEAD, z] = nothing

    def rise(e):
        return pltpu.make_async_remote_copy(
            src_ref=sent.at[e, planes - 1], dst_ref=below.at[e],
            send_sem=send_sem.at[e, 0], recv_sem=recv_sem.at[e, 0],
            device_id=(tm, sp + 1), device_id_type=MESH)

    def sink(e):
        return pltpu.make_async_remote_copy(
            src_ref=sent.at[e, 0], dst_ref=above.at[e],
            send_sem=send_sem.at[e, 1], recv_sem=recv_sem.at[e, 1],
            device_id=(tm, sp - 1), device_id_type=MESH)

    def post(e, role, u):
        for z in range(planes):
            sent[e, z] = own[1, dirs[role], z] * u[z]

        @pl.when(upper)
        def _():
            rise(e).start()

        @pl.when(lower)
        def _():
            sink(e).start()

    def arrive(e):
        @pl.when(lower)
        def _():
            rise(e).wait_recv()

        @pl.when(upper)
        def _():
            sink(e).wait_recv()

    at_dest = [1.0 - d.astype(jnp.float32) for d in dirs]
    at_src = [d.astype(jnp.float32) for d in dirs]
    hx, hy = 0.5 * drift_x, 0.5 * drift_y

    def advance(e, role, u, outs):
        d = dirs[role]
        dx, dy = at_dest[role] * hx, at_dest[role] * hy
        sx, sy = at_src[role] * hx, at_src[role] * hy
        rows, cols = u.shape[1:]
        for z in range(planes):
            v, w, a = u[z], sent[e, z], own[0, d, z]
            under = below[e] if z == 0 else sent[e, z - 1]
            over = above[e] if z == planes - 1 else sent[e, z + 1]
            vx, vy = sx * v, sy * v
            total = a * (under + over - 6.0 * w)
            total += (a - dx) * pltpu.roll(w + vx, cols - 1, 1)
            total += (a + dx) * pltpu.roll(w - vx, 1, 1)
            total += (a - dy) * pltpu.roll(w + vy, rows - 1, 0)
            total += (a + dy) * pltpu.roll(w - vy, 1, 0)
            for level, extra, dst in outs:
                dst[z] = v + tau_levels[level] * total + extra[z]

    def emit(direction, j):
        if direction == 0:
            dst = forward_out.at[j]
        else:
            dst = adjoint_out.at[steps - 1 - j]
        return pltpu.make_async_copy(points.at[direction, j], dst, out_sem.at[direction, j])

    def finish(role, j):
        @pl.when(dirs[role] == 0)
        def _():
            emit(0, j).start()

        @pl.when(dirs[role] == 1)
        def _():
            emit(1, j).start()

    def hand(slot, src, distance):
        return pltpu.make_async_remote_copy(
            src_ref=src, dst_ref=passed.at[slot],
            send_sem=pass_send.at[slot], recv_sem=pass_recv.at[slot],
            device_id=(tm + distance, sp), device_id_type=MESH)

    def forcing(role, j):
        return rhs.at[dirs[role], j]

    def point(role, j):
        return points.at[dirs[role], j]

    m1, m2, coarse, t_a1, t_a2 = [stage.at[i] for i in range(5)]

    def load(direction, j):
        fetch(direction, j).wait()
        if direction == 0:
            for z in range(planes):
                rhs[0, j, z] += push[j // 4, z]

    chains = [(HEAD, 0), (HEAD, 1), (TAIL, 0), (TAIL, 1)]
    for b in range(2):
        load(0, 4 * b)
        load(1, 4 * b)
    pl.semaphore_wait(barrier, count)
    for role, b in chains:
        post(fine_id(role, b, 0), role, forcing(role, 4 * b))
    for i in range(1, 4):
        for b in range(2):
            load(0, 4 * b + i)
            load(1, 4 * b + i)
    for i in range(3):
        for role, b in chains:
            e = fine_id(role, b, i)
            u = forcing(role, 4 * b) if i == 0 else march.at[role, b, i - 1]
            dst = resid.at[role, b] if i == 2 else march.at[role, b, i]
            arrive(e)
            advance(e, role, u, [(0, forcing(role, 4 * b + i + 1), dst)])
            if i < 2:
                post(e + 1, role, dst)
            elif (role, b) == (HEAD, 0):
                post(H_R1, HEAD, dst)
    h_r1, h_r2, t_r3, t_r4 = resid.at[HEAD, 0], resid.at[HEAD, 1], resid.at[TAIL, 0], resid.at[TAIL, 1]
    arrive(H_R1)
    advance(H_R1, HEAD, h_r1, [(1, h_r2, m1)])
    partner = sign_h
    hand(M1, m1, partner).start()
    hand(R1, h_r1, partner).start()
    hand(R2, h_r2, partner).start()
    hand(M1, m1, partner).wait_recv()
    post(T_M1, TAIL, passed.at[M1])
    arrive(T_M1)
    advance(T_M1, TAIL, passed.at[M1], [(1, t_r3, m2)])
    post(T_M2, TAIL, m2)
    arrive(T_M2)
    advance(T_M2, TAIL, m2, [(1, t_r4, coarse)])

    e_tail, e_head = passed.at[E_TAIL], passed.at[E_HEAD]
    h_a1, h_a2, t_a3, t_e = point(HEAD, 3), point(HEAD, 7), point(TAIL, 3), point(TAIL, 7)

    def relay():
        @pl.when(jnp.logical_not(last_t))
        def _():
            hand(E_TAIL, t_e, 2 * sign_t).start()
            hand(E_HEAD, t_e, sign_t).start()

    def tail0():
        @pl.when(first_t)
        def _():
            for z in range(planes):
                t_e[z] = coarse[z]
            relay()

        @pl.when(jnp.logical_not(first_t))
        def _():
            hand(E_TAIL, t_e, 2 * sign_t).wait_recv()
        post(T_E, TAIL, e_tail)
        arrive(T_E)

        @pl.when(jnp.logical_not(first_t))
        def _():
            advance(T_E, TAIL, e_tail, [(2, coarse, t_e)])
            relay()
        finish(TAIL, 7)

    def tail1():
        hand(R1, h_r1, partner).wait_recv()
        advance(T_E, TAIL, e_tail, [(1, passed.at[R1], t_a1)])
        post(T_A1, TAIL, t_a1)

    def tail2():
        arrive(T_A1)
        hand(R2, h_r2, partner).wait_recv()
        advance(T_A1, TAIL, t_a1, [(1, passed.at[R2], t_a2)])
        post(T_A2, TAIL, t_a2)

    def tail3():
        arrive(T_A2)
        advance(T_A2, TAIL, t_a2, [(1, t_r3, t_a3), (0, forcing(TAIL, 0), point(TAIL, 0))])
        post(T_A3, TAIL, t_a3)
        post(late_id(TAIL, 0, 0), TAIL, point(TAIL, 0))
        finish(TAIL, 3)
        finish(TAIL, 0)

    def late(role, b, i):
        e = late_id(role, b, i)
        j = 4 * b + i
        arrive(e)
        advance(e, role, point(role, j), [(0, forcing(role, j + 1), point(role, j + 1))])
        if i == 0:
            post(e + 1, role, point(role, j + 1))
        finish(role, j + 1)

    def tail4():
        arrive(T_A3)
        advance(T_A3, TAIL, t_a3, [(0, forcing(TAIL, 4), point(TAIL, 4))])
        post(late_id(TAIL, 1, 0), TAIL, point(TAIL, 4))
        finish(TAIL, 4)
        late(TAIL, 0, 0)

    def tail5():
        late(TAIL, 1, 0)
        late(TAIL, 0, 1)

    def tail6():
        late(TAIL, 1, 1)

    def head0():
        @pl.when(jnp.logical_not(first_h))
        def _():
            hand(E_HEAD, t_e, sign_t).wait_recv()
        post(H_E, HEAD, e_head)
        arrive(H_E)
        advance(H_E, HEAD, e_head, [(1, h_r1, h_a1), (0, forcing(HEAD, 0), point(HEAD, 0))])
        post(H_A1, HEAD, h_a1)
        post(late_id(HEAD, 0, 0), HEAD, point(HEAD, 0))
        finish(HEAD, 3)
        finish(HEAD, 0)

    def head1():
        arrive(H_A1)
        advance(H_A1, HEAD, h_a1, [(0, forcing(HEAD, 4), point(HEAD, 4)), (1, h_r2, h_a2)])
        post(late_id(HEAD, 1, 0), HEAD, point(HEAD, 4))
        finish(HEAD, 4)
        finish(HEAD, 7)
        late(HEAD, 0, 0)

    def head2():
        late(HEAD, 1, 0)
        late(HEAD, 0, 1)

    def head3():
        late(HEAD, 1, 1)

    head_first = g_h < g_t

    @pl.when(head_first)
    def _():
        for part in (head0, head1, tail0, tail1, head2, tail2, head3, tail3, tail4, tail5, tail6):
            part()

    @pl.when(jnp.logical_not(head_first))
    def _():
        for part in (tail0, tail1, tail2, tail3, tail4, head0, tail5, head1, tail6, head2, head3):
            part()

    def settle(e, carry):
        @pl.when(upper)
        def _():
            rise(e).wait_send()

        @pl.when(lower)
        def _():
            sink(e).wait_send()
        return carry

    lax.fori_loop(0, EXCHANGES, settle, 0)
    hand(M1, m1, partner).wait_send()
    hand(R1, h_r1, partner).wait_send()
    hand(R2, h_r2, partner).wait_send()

    @pl.when(jnp.logical_not(last_t))
    def _():
        hand(E_TAIL, t_e, 2 * sign_t).wait_send()
        hand(E_HEAD, t_e, sign_t).wait_send()
    for j in range(steps):
        emit(0, j).wait()
        emit(1, j).wait()


def solution(mesh):
    members, slabs = mesh.shape["tm"], mesh.shape["space"]

    def on_device(source, thrust_axial, thrust_lateral, yaw_index, diffusivity, cotangent):
        steps = source.shape[0]
        slab = diffusivity.shape
        plane = slab[1:]
        vmem = pl.BlockSpec(memory_space=pltpu.VMEM)
        anywhere = pl.BlockSpec(memory_space=pl.ANY)
        f32 = jnp.float32
        return pl.pallas_call(
            functools.partial(kernel, members, slabs),
            out_shape=(jax.ShapeDtypeStruct(source.shape, f32), jax.ShapeDtypeStruct(source.shape, f32)),
            in_specs=[pl.BlockSpec(memory_space=pltpu.SMEM), vmem, vmem, vmem, anywhere, anywhere],
            out_specs=(anywhere, anywhere),
            scratch_shapes=[
                pltpu.VMEM((2, steps) + slab, f32),
                pltpu.VMEM((2, steps) + slab, f32),
                pltpu.VMEM((EXCHANGES,) + slab, f32),
                pltpu.VMEM((EXCHANGES,) + plane, f32),
                pltpu.VMEM((EXCHANGES,) + plane, f32),
                pltpu.VMEM((2, 2) + slab, f32),
                pltpu.VMEM((2,) + slab, f32),
                pltpu.VMEM((2, 2, 2) + slab, f32),
                pltpu.VMEM((2, 2) + slab, f32),
                pltpu.VMEM((5,) + slab, f32),
                pltpu.VMEM((5,) + slab, f32),
                pltpu.SemaphoreType.DMA((EXCHANGES, 2)),
                pltpu.SemaphoreType.DMA((EXCHANGES, 2)),
                pltpu.SemaphoreType.DMA((5,)),
                pltpu.SemaphoreType.DMA((5,)),
                pltpu.SemaphoreType.DMA((2, steps)),
                pltpu.SemaphoreType.DMA((2, steps)),
            ],
            compiler_params=pltpu.CompilerParams(
                collective_id=0, has_side_effects=True, vmem_limit_bytes=40 * 1024 * 1024),
            cost_estimate=pl.CostEstimate(flops=40_000_000, bytes_accessed=4_500_000, transcendentals=0),
        )(yaw_index, thrust_axial, thrust_lateral, diffusivity, source, cotangent)

    return jax.shard_map(
        on_device,
        mesh=mesh,
        in_specs=(
            P("tm", "space", None, None),
            P("space", None, None),
            P("space", None, None),
            P("tm"),
            P("space", None, None),
            P("tm", "space", None, None),
        ),
        out_specs=(P("tm", "space", None, None), P("tm", "space", None, None)),
        check_vma=False,
    )
```

```python
import functools
import math

import jax
import jax.numpy as jnp
from jax import lax
from jax.experimental import pallas as pl
from jax.experimental.pallas import tpu as pltpu
from jax.sharding import PartitionSpec as P

YAWS = 24
MESH = pl.DeviceIdType.MESH

tau_levels = (0.03, 0.06, 0.08)
drift_x = 0.3
drift_y = 0.2

HEAD, TAIL = 0, 1
H_R1, T_M1, T_M2 = 12, 13, 14
T_E, T_A1, T_A2, T_A3 = 15, 16, 17, 18
H_E, H_A1 = 19, 20
FINE = 21
POWERS = 29
M1, R1, R2 = 0, 1, 2


def fine_id(role, block, step):
    return (role * 2 + block) * 3 + step


def late_id(role, block, step):
    return FINE + (role * 2 + block) * 2 + step


def kernel(
    members, slabs,
    yaw_hbm, axial_hbm, lateral_hbm, kappa_hbm, source, cotangent,
    forward_out, adjoint_out,
    yaw, axial, lateral, kappa, rhs, points, sent, below, above, own, push, march, resid, stage, passed, powers, parts,
    send_sem, recv_sem, pass_send, pass_recv, part_send, part_recv, in_sem, out_sem, small_sem,
):
    planes = kappa.shape[0]
    steps = source.shape[0]
    groups = members // 2
    exchanges = sent.shape[0]
    tm, sp = lax.axis_index("tm"), lax.axis_index("space")
    dir_h = lax.rem(tm, 2)
    dir_t = 1 - dir_h
    sign_h = 1 - 2 * dir_h
    sign_t = -sign_h
    pos_h = jnp.where(dir_h == 0, tm, members - 1 - tm)
    g_h = pos_h // 2
    g_t = groups - 1 - g_h
    dirs = (dir_h, dir_t)
    lower, upper = sp > 0, sp < slabs - 1
    neighbours = [(lower, tm, sp - 1), (upper, tm, sp + 1)]
    neighbours += [(tm != t, t, sp) for t in range(members)]
    barrier = pltpu.get_barrier_semaphore()
    count = 0
    for there, t, s in neighbours:
        count = count + there.astype(jnp.int32)

        @pl.when(there)
        def _():
            pl.semaphore_signal(barrier, inc=1, device_id=(t, s), device_id_type=MESH)

    def fetch(direction, j):
        if direction == 0:
            src = source.at[j]
        else:
            src = cotangent.at[steps - 1 - j]
        return pltpu.make_async_copy(src, rhs.at[direction, j], in_sem.at[direction, j])

    small = [
        pltpu.make_async_copy(src, dst, small_sem.at[i])
        for i, (src, dst) in enumerate(
            ((yaw_hbm, yaw), (kappa_hbm, kappa), (axial_hbm, axial), (lateral_hbm, lateral)))
    ]
    for copy in small:
        copy.start()
    for i in range(4):
        for b in range(2):
            fetch(0, 4 * b + i).start()
            fetch(1, 4 * b + i).start()

    nothing = jnp.zeros(below.shape[1:], jnp.float32)

    @pl.when(jnp.logical_not(lower))
    def _():
        def clear(e, carry):
            below[e] = nothing
            return carry
        lax.fori_loop(0, exchanges, clear, 0)

    @pl.when(jnp.logical_not(upper))
    def _():
        def clear(e, carry):
            above[e] = nothing
            return carry
        lax.fori_loop(0, exchanges, clear, 0)

    for copy in small:
        copy.wait()
    ones = jnp.ones(kappa.shape, jnp.float32)
    own[0, 0] = kappa[...]
    own[0, 1] = ones
    own[1, 0] = ones
    own[1, 1] = kappa[...]
    for b in range(2):
        angle = (2.0 * math.pi / YAWS) * jnp.full(kappa.shape[1:], yaw[b], jnp.int32).astype(jnp.float32)
        c, s = jnp.cos(angle[:8]), jnp.sin(angle[:8])
        reps = kappa.shape[1] // 8
        c, s = jnp.concatenate([c] * reps, 0), jnp.concatenate([s] * reps, 0)
        for z in range(planes):
            push[b, z] = c * axial[z] + s * lateral[z]

    def rise(e):
        return pltpu.make_async_remote_copy(
            src_ref=sent.at[e, planes - 1], dst_ref=below.at[e],
            send_sem=send_sem.at[e, 0], recv_sem=recv_sem.at[e, 0],
            device_id=(tm, sp + 1), device_id_type=MESH)

    def sink(e):
        return pltpu.make_async_remote_copy(
            src_ref=sent.at[e, 0], dst_ref=above.at[e],
            send_sem=send_sem.at[e, 1], recv_sem=recv_sem.at[e, 1],
            device_id=(tm, sp - 1), device_id_type=MESH)

    def post(e, role, u):
        for z in range(planes):
            sent[e, z] = own[1, dirs[role], z] * u[z]

        @pl.when(upper)
        def _():
            rise(e).start()

        @pl.when(lower)
        def _():
            sink(e).start()

    def arrive(e):
        @pl.when(lower)
        def _():
            rise(e).wait_recv()

        @pl.when(upper)
        def _():
            sink(e).wait_recv()

    at_dest = [1.0 - d.astype(jnp.float32) for d in dirs]
    at_src = [d.astype(jnp.float32) for d in dirs]
    hx, hy = 0.5 * drift_x, 0.5 * drift_y

    def advance(e, role, u, outs):
        d = dirs[role]
        dx, dy = at_dest[role] * hx, at_dest[role] * hy
        sx, sy = at_src[role] * hx, at_src[role] * hy
        rows, cols = u.shape[1:]
        for z in range(planes):
            v, w, a = u[z], sent[e, z], own[0, d, z]
            under = below[e] if z == 0 else sent[e, z - 1]
            over = above[e] if z == planes - 1 else sent[e, z + 1]
            vx, vy = sx * v, sy * v
            total = a * (under + over - 6.0 * w)
            total += (a - dx) * pltpu.roll(w + vx, cols - 1, 1)
            total += (a + dx) * pltpu.roll(w - vx, 1, 1)
            total += (a - dy) * pltpu.roll(w + vy, rows - 1, 0)
            total += (a + dy) * pltpu.roll(w - vy, 1, 0)
            for level, extra, dst in outs:
                value = v + tau_levels[level] * total
                dst[z] = value if extra is None else value + extra[z]

    def emit(direction, j):
        if direction == 0:
            dst = forward_out.at[j]
        else:
            dst = adjoint_out.at[steps - 1 - j]
        return pltpu.make_async_copy(points.at[direction, j], dst, out_sem.at[direction, j])

    def finish(role, j):
        @pl.when(dirs[role] == 0)
        def _():
            emit(0, j).start()

        @pl.when(dirs[role] == 1)
        def _():
            emit(1, j).start()

    def hand(slot, src, distance):
        return pltpu.make_async_remote_copy(
            src_ref=src, dst_ref=passed.at[slot],
            send_sem=pass_send.at[slot], recv_sem=pass_recv.at[slot],
            device_id=(tm + distance, sp), device_id_type=MESH)

    def forcing(role, j):
        return rhs.at[dirs[role], j]

    def point(role, j):
        return points.at[dirs[role], j]

    m1, m2, t_a1, t_a2, e_head, e_tail = [stage.at[i] for i in range(6)]
    coarse = powers.at[0]

    def load(direction, j):
        fetch(direction, j).wait()
        if direction == 0:
            for z in range(planes):
                rhs[0, j, z] += push[j // 4, z]

    chains = [(HEAD, 0), (HEAD, 1), (TAIL, 0), (TAIL, 1)]
    for b in range(2):
        load(0, 4 * b)
        load(1, 4 * b)
    pl.semaphore_wait(barrier, count)
    for role, b in chains:
        post(fine_id(role, b, 0), role, forcing(role, 4 * b))
    for i in range(1, 4):
        for b in range(2):
            load(0, 4 * b + i)
            load(1, 4 * b + i)
    for i in range(3):
        for role, b in chains:
            e = fine_id(role, b, i)
            u = forcing(role, 4 * b) if i == 0 else march.at[role, b, i - 1]
            dst = resid.at[role, b] if i == 2 else march.at[role, b, i]
            arrive(e)
            advance(e, role, u, [(0, forcing(role, 4 * b + i + 1), dst)])
            if i < 2:
                post(e + 1, role, dst)
            elif (role, b) == (HEAD, 0):
                post(H_R1, HEAD, dst)
    h_r1, h_r2, t_r3, t_r4 = resid.at[HEAD, 0], resid.at[HEAD, 1], resid.at[TAIL, 0], resid.at[TAIL, 1]
    arrive(H_R1)
    advance(H_R1, HEAD, h_r1, [(1, h_r2, m1)])
    partner = sign_h
    hand(M1, m1, partner).start()
    hand(R1, h_r1, partner).start()
    hand(R2, h_r2, partner).start()
    hand(M1, m1, partner).wait_recv()
    post(T_M1, TAIL, passed.at[M1])
    arrive(T_M1)
    advance(T_M1, TAIL, passed.at[M1], [(1, t_r3, m2)])
    post(T_M2, TAIL, m2)
    arrive(T_M2)
    advance(T_M2, TAIL, m2, [(1, t_r4, coarse)])

    h_a1, h_a2, t_a3, t_e = point(HEAD, 3), point(HEAD, 7), point(TAIL, 3), point(TAIL, 7)

    def part(role, i):
        return pltpu.make_async_remote_copy(
            src_ref=powers.at[i], dst_ref=parts.at[role, i],
            send_sem=part_send.at[role, i], recv_sem=part_recv.at[role, i],
            device_id=(tm + sign_t * (2 * i + 1 + role), sp), device_id_type=MESH)

    for i in range(groups - 1):
        @pl.when(g_t + 1 + i < groups)
        def _():
            if i > 0:
                e = POWERS + i - 1
                post(e, TAIL, powers.at[i - 1])
                arrive(e)
                advance(e, TAIL, powers.at[i - 1], [(2, None, powers.at[i])])
            part(TAIL, i).start()
            part(HEAD, i).start()

    def gather(role, group, total):
        for z in range(planes):
            total[z] = jnp.zeros(total.shape[1:], jnp.float32)
        for i in range(groups - 1):
            @pl.when(i < group)
            def _():
                part(role, i).wait_recv()
                for z in range(planes):
                    total[z] += parts[role, i, z]

    def tail0():
        gather(TAIL, g_t, e_tail)
        post(T_E, TAIL, e_tail)

    def tail1():
        arrive(T_E)
        hand(R1, h_r1, partner).wait_recv()
        advance(T_E, TAIL, e_tail, [(1, passed.at[R1], t_a1), (2, coarse, t_e)])
        post(T_A1, TAIL, t_a1)
        finish(TAIL, 7)

    def tail2():
        arrive(T_A1)
        hand(R2, h_r2, partner).wait_recv()
        advance(T_A1, TAIL, t_a1, [(1, passed.at[R2], t_a2)])
        post(T_A2, TAIL, t_a2)

    def tail3():
        arrive(T_A2)
        advance(T_A2, TAIL, t_a2, [(1, t_r3, t_a3), (0, forcing(TAIL, 0), point(TAIL, 0))])
        post(T_A3, TAIL, t_a3)
        post(late_id(TAIL, 0, 0), TAIL, point(TAIL, 0))
        finish(TAIL, 3)
        finish(TAIL, 0)

    def late(role, b, i):
        e = late_id(role, b, i)
        j = 4 * b + i
        arrive(e)
        advance(e, role, point(role, j), [(0, forcing(role, j + 1), point(role, j + 1))])
        if i == 0:
            post(e + 1, role, point(role, j + 1))
        finish(role, j + 1)

    def tail4():
        arrive(T_A3)
        advance(T_A3, TAIL, t_a3, [(0, forcing(TAIL, 4), point(TAIL, 4))])
        post(late_id(TAIL, 1, 0), TAIL, point(TAIL, 4))
        finish(TAIL, 4)
        late(TAIL, 0, 0)

    def tail5():
        late(TAIL, 1, 0)
        late(TAIL, 0, 1)

    def tail6():
        late(TAIL, 1, 1)

    def head0():
        gather(HEAD, g_h, e_head)
        post(H_E, HEAD, e_head)

    def head1():
        arrive(H_E)
        advance(H_E, HEAD, e_head, [(1, h_r1, h_a1), (0, forcing(HEAD, 0), point(HEAD, 0))])
        post(H_A1, HEAD, h_a1)
        post(late_id(HEAD, 0, 0), HEAD, point(HEAD, 0))
        finish(HEAD, 3)
        finish(HEAD, 0)

    def head2():
        arrive(H_A1)
        advance(H_A1, HEAD, h_a1, [(0, forcing(HEAD, 4), point(HEAD, 4)), (1, h_r2, h_a2)])
        post(late_id(HEAD, 1, 0), HEAD, point(HEAD, 4))
        finish(HEAD, 4)
        finish(HEAD, 7)
        late(HEAD, 0, 0)

    def head3():
        late(HEAD, 1, 0)
        late(HEAD, 0, 1)

    def head4():
        late(HEAD, 1, 1)

    head_first = g_h < g_t

    @pl.when(head_first)
    def _():
        for part in (head0, head1, tail0, tail1, head2, tail2, head3, tail3, head4, tail4, tail5, tail6):
            part()

    @pl.when(jnp.logical_not(head_first))
    def _():
        for part in (tail0, tail1, tail2, head0, head1, tail3, head2, tail4, head3, tail5, head4, tail6):
            part()

    def settle(e, carry):
        @pl.when(upper)
        def _():
            rise(e).wait_send()

        @pl.when(lower)
        def _():
            sink(e).wait_send()
        return carry

    lax.fori_loop(0, POWERS, settle, 0)
    hand(M1, m1, partner).wait_send()
    hand(R1, h_r1, partner).wait_send()
    hand(R2, h_r2, partner).wait_send()

    for i in range(groups - 1):
        @pl.when(g_t + 1 + i < groups)
        def _():
            part(TAIL, i).wait_send()
            part(HEAD, i).wait_send()
            if i > 0:
                settle(POWERS + i - 1, 0)
    for j in range(steps):
        emit(0, j).wait()
        emit(1, j).wait()


def solution(mesh):
    members, slabs = mesh.shape["tm"], mesh.shape["space"]

    def on_device(source, thrust_axial, thrust_lateral, yaw_index, diffusivity, cotangent):
        steps = source.shape[0]
        links = members // 2 - 1
        exchanges = POWERS + links - 1
        slab = diffusivity.shape
        plane = slab[1:]
        anywhere = pl.BlockSpec(memory_space=pl.ANY)
        f32 = jnp.float32
        return pl.pallas_call(
            functools.partial(kernel, members, slabs),
            out_shape=(jax.ShapeDtypeStruct(source.shape, f32), jax.ShapeDtypeStruct(source.shape, f32)),
            in_specs=[anywhere] * 6,
            out_specs=(anywhere, anywhere),
            scratch_shapes=[
                pltpu.SMEM(yaw_index.shape, jnp.int32),
                pltpu.VMEM(slab, f32),
                pltpu.VMEM(slab, f32),
                pltpu.VMEM(slab, f32),
                pltpu.VMEM((2, steps) + slab, f32),
                pltpu.VMEM((2, steps) + slab, f32),
                pltpu.VMEM((exchanges,) + slab, f32),
                pltpu.VMEM((exchanges,) + plane, f32),
                pltpu.VMEM((exchanges,) + plane, f32),
                pltpu.VMEM((2, 2) + slab, f32),
                pltpu.VMEM((2,) + slab, f32),
                pltpu.VMEM((2, 2, 2) + slab, f32),
                pltpu.VMEM((2, 2) + slab, f32),
                pltpu.VMEM((6,) + slab, f32),
                pltpu.VMEM((3,) + slab, f32),
                pltpu.VMEM((links,) + slab, f32),
                pltpu.VMEM((2, links) + slab, f32),
                pltpu.SemaphoreType.DMA((exchanges, 2)),
                pltpu.SemaphoreType.DMA((exchanges, 2)),
                pltpu.SemaphoreType.DMA((3,)),
                pltpu.SemaphoreType.DMA((3,)),
                pltpu.SemaphoreType.DMA((2, links)),
                pltpu.SemaphoreType.DMA((2, links)),
                pltpu.SemaphoreType.DMA((2, steps)),
                pltpu.SemaphoreType.DMA((2, steps)),
                pltpu.SemaphoreType.DMA((4,)),
            ],
            compiler_params=pltpu.CompilerParams(
                collective_id=0, has_side_effects=True, vmem_limit_bytes=60 * 1024 * 1024),
            cost_estimate=pl.CostEstimate(flops=40_000_000, bytes_accessed=4_500_000, transcendentals=0),
        )(yaw_index, thrust_axial, thrust_lateral, diffusivity, source, cotangent)

    return jax.shard_map(
        on_device,
        mesh=mesh,
        in_specs=(
            P("tm", "space", None, None),
            P("space", None, None),
            P("space", None, None),
            P("tm"),
            P("space", None, None),
            P("tm", "space", None, None),
        ),
        out_specs=(P("tm", "space", None, None), P("tm", "space", None, None)),
        check_vma=False,
    )
```

```python
import functools
import math

import jax
import jax.numpy as jnp
from jax import lax
from jax.experimental import pallas as pl
from jax.experimental.pallas import tpu as pltpu
from jax.sharding import PartitionSpec as P

YAWS = 24
MESH = pl.DeviceIdType.MESH

tau_levels = (0.03, 0.06, 0.08)
drift_x = 0.3
drift_y = 0.2

HEAD, TAIL = 0, 1
KAPPA, H_R1, T_R3, T_R1, T_M1, T_E, H_E, T_A2 = range(12, 20)
FIFTH, LATE, POWERS = 20, 22, 26
PAD = 2
M1, R1, R2 = 0, 1, 2


def fine_id(role, block, step):
    return (role * 2 + block) * 3 + step


def kernel(
    members, slabs,
    yaw_hbm, axial_hbm, lateral_hbm, kappa_hbm, source, cotangent,
    forward_out, adjoint_out,
    yaw, axial, lateral, kappa, rhs, points, own, push, march, resid, stage, passed, powers, parts,
    send_sem, recv_sem, pass_send, pass_recv, part_send, part_recv, in_sem, out_sem, small_sem,
):
    planes = kappa.shape[0]
    steps = source.shape[0]
    groups = members // 2
    mid = slice(PAD, PAD + planes)
    mine = pl.ds(PAD, planes)
    tm, sp = lax.axis_index("tm"), lax.axis_index("space")
    dir_h = lax.rem(tm, 2)
    dir_t = 1 - dir_h
    sign_h = 1 - 2 * dir_h
    sign_t = -sign_h
    pos_h = jnp.where(dir_h == 0, tm, members - 1 - tm)
    g_h = pos_h // 2
    g_t = groups - 1 - g_h
    dirs = (dir_h, dir_t)
    lower, upper = sp > 0, sp < slabs - 1
    neighbours = [(lower, tm, sp - 1), (upper, tm, sp + 1)]
    neighbours += [(tm != t, t, sp) for t in range(members)]
    barrier = pltpu.get_barrier_semaphore()
    count = 0
    for there, t, s in neighbours:
        count = count + there.astype(jnp.int32)

        @pl.when(there)
        def _():
            pl.semaphore_signal(barrier, inc=1, device_id=(t, s), device_id_type=MESH)

    def fetch(direction, j):
        if direction == 0:
            src = source.at[j]
        else:
            src = cotangent.at[steps - 1 - j]
        return pltpu.make_async_copy(src, rhs.at[direction, j, mine], in_sem.at[direction, j])

    small = [
        pltpu.make_async_copy(src, dst, small_sem.at[i])
        for i, (src, dst) in enumerate(
            ((yaw_hbm, yaw), (kappa_hbm, kappa), (axial_hbm, axial), (lateral_hbm, lateral)))
    ]
    for copy in small:
        copy.start()
    for i in range(4):
        for b in range(2):
            fetch(0, 4 * b + i).start()
            fetch(1, 4 * b + i).start()

    for copy in small:
        copy.wait()
    wide = own.shape[2:]
    own[0, 1] = jnp.ones(wide, jnp.float32)
    own[1, 0] = jnp.ones(wide, jnp.float32)
    diffuse = own.at[1, 1]
    diffuse[mid] = kappa[...]
    for b in range(2):
        angle = (2.0 * math.pi / YAWS) * jnp.full(kappa.shape[1:], yaw[b], jnp.int32).astype(jnp.float32)
        c, s = jnp.cos(angle[:8]), jnp.sin(angle[:8])
        reps = kappa.shape[1] // 8
        c, s = jnp.concatenate([c] * reps, 0), jnp.concatenate([s] * reps, 0)
        for z in range(planes):
            push[b, z] = c * axial[z] + s * lateral[z]

    def rise(e, ref, depth):
        return pltpu.make_async_remote_copy(
            src_ref=ref.at[pl.ds(PAD + planes - depth, depth)], dst_ref=ref.at[pl.ds(PAD - depth, depth)],
            send_sem=send_sem.at[e, 0], recv_sem=recv_sem.at[e, 0],
            device_id=(tm, sp + 1), device_id_type=MESH)

    def sink(e, ref, depth):
        return pltpu.make_async_remote_copy(
            src_ref=ref.at[pl.ds(PAD, depth)], dst_ref=ref.at[pl.ds(PAD + planes, depth)],
            send_sem=send_sem.at[e, 1], recv_sem=recv_sem.at[e, 1],
            device_id=(tm, sp - 1), device_id_type=MESH)

    posted = {}

    def post(e, ref, depth):
        posted[e] = (ref, depth)
        none = jnp.zeros((depth,) + ref.shape[1:], jnp.float32)

        @pl.when(upper)
        def _():
            rise(e, ref, depth).start()

        @pl.when(jnp.logical_not(upper))
        def _():
            ref[PAD + planes:PAD + planes + depth] = none

        @pl.when(lower)
        def _():
            sink(e, ref, depth).start()

        @pl.when(jnp.logical_not(lower))
        def _():
            ref[PAD - depth:PAD] = none

    def arrive(e):
        ref, depth = posted[e]

        @pl.when(lower)
        def _():
            rise(e, ref, depth).wait_recv()

        @pl.when(upper)
        def _():
            sink(e, ref, depth).wait_recv()

    at_dest = [1.0 - d.astype(jnp.float32) for d in dirs]
    at_src = [d.astype(jnp.float32) for d in dirs]
    hx, hy = 0.5 * drift_x, 0.5 * drift_y

    def advance(role, u, outs, reach=0):
        d = dirs[role]
        dx, dy = at_dest[role] * hx, at_dest[role] * hy
        sx, sy = at_src[role] * hx, at_src[role] * hy
        rows, cols = u.shape[1:]
        for z in range(PAD - reach, PAD + planes + reach):
            v, a = u[z], own[0, d, z]
            w = own[1, d, z] * v
            under = own[1, d, z - 1] * u[z - 1]
            over = own[1, d, z + 1] * u[z + 1]
            vx, vy = sx * v, sy * v
            total = a * (under + over - 6.0 * w)
            total += (a - dx) * pltpu.roll(w + vx, cols - 1, 1)
            total += (a + dx) * pltpu.roll(w - vx, 1, 1)
            total += (a - dy) * pltpu.roll(w + vy, rows - 1, 0)
            total += (a + dy) * pltpu.roll(w - vy, 1, 0)
            for level, extra, dst in outs:
                value = v + tau_levels[level] * total
                dst[z] = value if extra is None else value + extra[z]

    def emit(direction, j):
        if direction == 0:
            dst = forward_out.at[j]
        else:
            dst = adjoint_out.at[steps - 1 - j]
        return pltpu.make_async_copy(points.at[direction, j, mine], dst, out_sem.at[direction, j])

    def finish(role, j):
        @pl.when(dirs[role] == 0)
        def _():
            emit(0, j).start()

        @pl.when(dirs[role] == 1)
        def _():
            emit(1, j).start()

    def hand(slot, src, distance):
        return pltpu.make_async_remote_copy(
            src_ref=src.at[mine], dst_ref=passed.at[slot, mine],
            send_sem=pass_send.at[slot], recv_sem=pass_recv.at[slot],
            device_id=(tm + distance, sp), device_id_type=MESH)

    def forcing(role, j):
        return rhs.at[dirs[role], j]

    def point(role, j):
        return points.at[dirs[role], j]

    m1, m2, t_a1, t_a2, e_head, e_tail = [stage.at[i] for i in range(6)]
    coarse = powers.at[0]

    def load(direction, j):
        fetch(direction, j).wait()
        if direction == 0:
            for z in range(planes):
                rhs[0, j, PAD + z] += push[j // 4, z]

    chains = [(HEAD, 0), (HEAD, 1), (TAIL, 0), (TAIL, 1)]
    for b in range(2):
        load(0, 4 * b)
        load(1, 4 * b)
    pl.semaphore_wait(barrier, count)
    post(KAPPA, diffuse, 2)
    for role, b in chains:
        post(fine_id(role, b, 0), forcing(role, 4 * b), 1)
    for i in range(1, 4):
        for b in range(2):
            load(0, 4 * b + i)
            load(1, 4 * b + i)
    arrive(KAPPA)
    own[0, 0] = diffuse[...]
    for i in range(3):
        for role, b in chains:
            e = fine_id(role, b, i)
            u = forcing(role, 4 * b) if i == 0 else march.at[role, b, i - 1]
            dst = resid.at[role, b] if i == 2 else march.at[role, b, i]
            arrive(e)
            advance(role, u, [(0, forcing(role, 4 * b + i + 1), dst)])
            if i < 2:
                post(e + 1, dst, 1)
            elif b == 0:
                post(H_R1 if role == HEAD else T_R3, dst, 1)
    h_r1, h_r2, t_r3, t_r4 = resid.at[HEAD, 0], resid.at[HEAD, 1], resid.at[TAIL, 0], resid.at[TAIL, 1]
    t_m1, t_r1, t_r2 = passed.at[M1], passed.at[R1], passed.at[R2]
    partner = sign_h
    arrive(H_R1)
    advance(HEAD, h_r1, [(1, h_r2, m1)])
    hand(M1, m1, partner).start()
    hand(R1, h_r1, partner).start()
    hand(R2, h_r2, partner).start()
    for role in (HEAD, TAIL):
        post(FIFTH + role, forcing(role, 5), 1)
    arrive(T_R3)
    hand(M1, m1, partner).wait_recv()
    post(T_M1, t_m1, 2)
    arrive(T_M1)
    advance(TAIL, t_m1, [(1, t_r3, m2)], 1)
    advance(TAIL, m2, [(1, t_r4, coarse)])

    h_a1, h_a2, t_a3, t_e = point(HEAD, 3), point(HEAD, 7), point(TAIL, 3), point(TAIL, 7)

    def part(role, i):
        return pltpu.make_async_remote_copy(
            src_ref=powers.at[i, mine], dst_ref=parts.at[role, i],
            send_sem=part_send.at[role, i], recv_sem=part_recv.at[role, i],
            device_id=(tm + sign_t * (2 * i + 1 + role), sp), device_id_type=MESH)

    for i in range(groups - 1):
        @pl.when(g_t + 1 + i < groups)
        def _():
            if i % 2 == 1:
                e = POWERS + i // 2
                post(e, powers.at[i - 1], 2)
                arrive(e)
                advance(TAIL, powers.at[i - 1], [(2, None, powers.at[i])], 1)
            elif i > 0:
                advance(TAIL, powers.at[i - 1], [(2, None, powers.at[i])])
            part(TAIL, i).start()
            part(HEAD, i).start()

    hand(R1, h_r1, partner).wait_recv()
    post(T_R1, t_r1, 1)

    def gather(role, group, total):
        total[mid] = jnp.zeros((planes,) + total.shape[1:], jnp.float32)
        for i in range(groups - 1):
            @pl.when(i < group)
            def _():
                part(role, i).wait_recv()
                for z in range(planes):
                    total[PAD + z] += parts[role, i, z]

    def tail0():
        gather(TAIL, g_t, e_tail)
        post(T_E, e_tail, 2)

    def tail1():
        arrive(T_R1)
        hand(R2, h_r2, partner).wait_recv()
        arrive(T_E)
        advance(TAIL, e_tail, [(1, t_r1, t_a1)], 1)
        advance(TAIL, t_a1, [(1, t_r2, t_a2)])
        post(T_A2, t_a2, 2)
        advance(TAIL, e_tail, [(2, coarse, t_e)])
        finish(TAIL, 7)

    def tail2():
        arrive(FIFTH + TAIL)
        arrive(T_A2)
        advance(TAIL, t_a2, [(1, t_r3, t_a3), (0, forcing(TAIL, 0), point(TAIL, 0))], 1)
        advance(TAIL, t_a3, [(0, forcing(TAIL, 4), point(TAIL, 4))])
        post(LATE + TAIL * 2, point(TAIL, 4), 2)
        advance(TAIL, point(TAIL, 0), [(0, forcing(TAIL, 1), point(TAIL, 1))])
        post(LATE + TAIL * 2 + 1, point(TAIL, 1), 1)
        for j in (3, 0, 4, 1):
            finish(TAIL, j)

    def last(role):
        arrive(LATE + role * 2)
        advance(role, point(role, 4), [(0, forcing(role, 5), point(role, 5))], 1)
        advance(role, point(role, 5), [(0, forcing(role, 6), point(role, 6))])
        finish(role, 5)
        finish(role, 6)
        arrive(LATE + role * 2 + 1)
        advance(role, point(role, 1), [(0, forcing(role, 2), point(role, 2))])
        finish(role, 2)

    def tail3():
        last(TAIL)

    def head0():
        gather(HEAD, g_h, e_head)
        post(H_E, e_head, 2)

    def head1():
        arrive(FIFTH + HEAD)
        arrive(H_E)
        advance(HEAD, e_head, [(1, h_r1, h_a1), (0, forcing(HEAD, 0), point(HEAD, 0))], 1)
        advance(HEAD, h_a1, [(0, forcing(HEAD, 4), point(HEAD, 4)), (1, h_r2, h_a2)])
        post(LATE + HEAD * 2, point(HEAD, 4), 2)
        advance(HEAD, point(HEAD, 0), [(0, forcing(HEAD, 1), point(HEAD, 1))])
        post(LATE + HEAD * 2 + 1, point(HEAD, 1), 1)
        for j in (3, 0, 4, 7, 1):
            finish(HEAD, j)

    def head2():
        last(HEAD)

    head_first = g_h < g_t

    @pl.when(head_first)
    def _():
        for piece in (head0, head1, tail0, tail1, head2, tail2, tail3):
            piece()

    @pl.when(jnp.logical_not(head_first))
    def _():
        for piece in (tail0, tail1, head0, tail2, head1, tail3, head2):
            piece()

    def settle(e, ref, depth):

        @pl.when(upper)
        def _():
            rise(e, ref, depth).wait_send()

        @pl.when(lower)
        def _():
            sink(e, ref, depth).wait_send()

    for e in range(LATE):
        settle(e, *posted[e])
    for role in (HEAD, TAIL):
        settle(LATE + role * 2, point(role, 4), 2)
        settle(LATE + role * 2 + 1, point(role, 1), 1)
    hand(M1, m1, partner).wait_send()
    hand(R1, h_r1, partner).wait_send()
    hand(R2, h_r2, partner).wait_send()

    for i in range(groups - 1):
        @pl.when(g_t + 1 + i < groups)
        def _():
            part(TAIL, i).wait_send()
            part(HEAD, i).wait_send()
            if i % 2 == 1:
                settle(POWERS + i // 2, powers.at[i - 1], 2)
    for j in range(steps):
        emit(0, j).wait()
        emit(1, j).wait()


def solution(mesh):
    members, slabs = mesh.shape["tm"], mesh.shape["space"]

    def on_device(source, thrust_axial, thrust_lateral, yaw_index, diffusivity, cotangent):
        steps = source.shape[0]
        links = members // 2 - 1
        exchanges = POWERS + max(1, links // 2)
        slab = diffusivity.shape
        wide = (slab[0] + 2 * PAD,) + slab[1:]
        anywhere = pl.BlockSpec(memory_space=pl.ANY)
        f32 = jnp.float32
        return pl.pallas_call(
            functools.partial(kernel, members, slabs),
            out_shape=(jax.ShapeDtypeStruct(source.shape, f32), jax.ShapeDtypeStruct(source.shape, f32)),
            in_specs=[anywhere] * 6,
            out_specs=(anywhere, anywhere),
            scratch_shapes=[
                pltpu.SMEM(yaw_index.shape, jnp.int32),
                pltpu.VMEM(slab, f32),
                pltpu.VMEM(slab, f32),
                pltpu.VMEM(slab, f32),
                pltpu.VMEM((2, steps) + wide, f32),
                pltpu.VMEM((2, steps) + wide, f32),
                pltpu.VMEM((2, 2) + wide, f32),
                pltpu.VMEM((2,) + slab, f32),
                pltpu.VMEM((2, 2, 2) + wide, f32),
                pltpu.VMEM((2, 2) + wide, f32),
                pltpu.VMEM((6,) + wide, f32),
                pltpu.VMEM((3,) + wide, f32),
                pltpu.VMEM((links,) + wide, f32),
                pltpu.VMEM((2, links) + slab, f32),
                pltpu.SemaphoreType.DMA((exchanges, 2)),
                pltpu.SemaphoreType.DMA((exchanges, 2)),
                pltpu.SemaphoreType.DMA((3,)),
                pltpu.SemaphoreType.DMA((3,)),
                pltpu.SemaphoreType.DMA((2, links)),
                pltpu.SemaphoreType.DMA((2, links)),
                pltpu.SemaphoreType.DMA((2, steps)),
                pltpu.SemaphoreType.DMA((2, steps)),
                pltpu.SemaphoreType.DMA((4,)),
            ],
            compiler_params=pltpu.CompilerParams(
                collective_id=0, has_side_effects=True, vmem_limit_bytes=60 * 1024 * 1024),
            cost_estimate=pl.CostEstimate(flops=40_000_000, bytes_accessed=4_500_000, transcendentals=0),
        )(yaw_index, thrust_axial, thrust_lateral, diffusivity, source, cotangent)

    return jax.shard_map(
        on_device,
        mesh=mesh,
        in_specs=(
            P("tm", "space", None, None),
            P("space", None, None),
            P("space", None, None),
            P("tm"),
            P("space", None, None),
            P("tm", "space", None, None),
        ),
        out_specs=(P("tm", "space", None, None), P("tm", "space", None, None)),
        check_vma=False,
    )
```

```python
import functools
import math

import jax
import jax.numpy as jnp
from jax import lax
from jax.experimental import pallas as pl
from jax.experimental.pallas import tpu as pltpu
from jax.sharding import PartitionSpec as P

YAWS = 24
MESH = pl.DeviceIdType.MESH

tau_levels = (0.03, 0.06, 0.08)
drift_x = 0.3
drift_y = 0.2

HEAD, TAIL = 0, 1
KAPPA, H_R1, T_R3, T_R1, T_M1, T_E, H_E, T_A2 = range(12, 20)
FIFTH, LATE, POWERS = 20, 22, 26
PAD = 2
M1, R1, R2, E_HEAD = 0, 1, 2, 3


def fine_id(role, block, step):
    return (role * 2 + block) * 3 + step


def kernel(
    members, slabs,
    yaw_hbm, axial_hbm, lateral_hbm, kappa_hbm, source, cotangent,
    forward_out, adjoint_out,
    yaw, axial, lateral, kappa, rhs, points, own, push, march, resid, stage, passed, powers, parts,
    send_sem, recv_sem, pass_send, pass_recv, part_send, part_recv, in_sem, out_sem, small_sem,
):
    planes = kappa.shape[0]
    steps = source.shape[0]
    groups = members // 2
    mid = slice(PAD, PAD + planes)
    mine = pl.ds(PAD, planes)
    tm, sp = lax.axis_index("tm"), lax.axis_index("space")
    dir_h = lax.rem(tm, 2)
    dir_t = 1 - dir_h
    sign_h = 1 - 2 * dir_h
    sign_t = -sign_h
    pos_h = jnp.where(dir_h == 0, tm, members - 1 - tm)
    g_h = pos_h // 2
    g_t = groups - 1 - g_h
    dirs = (dir_h, dir_t)
    lower, upper = sp > 0, sp < slabs - 1
    neighbours = [(lower, tm, sp - 1), (upper, tm, sp + 1)]
    for t in range(members):
        alike = jnp.logical_and(lax.rem(tm + t, 2) == 0, tm != t)
        neighbours.append((jnp.logical_or(alike, tm + sign_h == t), t, sp))
    barrier = pltpu.get_barrier_semaphore()
    count = 0
    for there, t, s in neighbours:
        count = count + there.astype(jnp.int32)

        @pl.when(there)
        def _():
            pl.semaphore_signal(barrier, inc=1, device_id=(t, s), device_id_type=MESH)

    def fetch(direction, j):
        if direction == 0:
            src = source.at[j]
        else:
            src = cotangent.at[steps - 1 - j]
        return pltpu.make_async_copy(src, rhs.at[direction, j, mine], in_sem.at[direction, j])

    small = [
        pltpu.make_async_copy(src, dst, small_sem.at[i])
        for i, (src, dst) in enumerate(
            ((yaw_hbm, yaw), (kappa_hbm, kappa), (axial_hbm, axial), (lateral_hbm, lateral)))
    ]
    for copy in small:
        copy.start()
    for i in range(4):
        for b in range(2):
            fetch(0, 4 * b + i).start()
            fetch(1, 4 * b + i).start()

    for copy in small:
        copy.wait()
    wide = own.shape[2:]
    own[0, 1] = jnp.ones(wide, jnp.float32)
    own[1, 0] = jnp.ones(wide, jnp.float32)
    diffuse = own.at[1, 1]
    diffuse[mid] = kappa[...]
    for b in range(2):
        angle = (2.0 * math.pi / YAWS) * jnp.full(kappa.shape[1:], yaw[b], jnp.int32).astype(jnp.float32)
        c, s = jnp.cos(angle[:8]), jnp.sin(angle[:8])
        reps = kappa.shape[1] // 8
        c, s = jnp.concatenate([c] * reps, 0), jnp.concatenate([s] * reps, 0)
        for z in range(planes):
            push[b, z] = c * axial[z] + s * lateral[z]

    def rise(e, ref, depth):
        return pltpu.make_async_remote_copy(
            src_ref=ref.at[pl.ds(PAD + planes - depth, depth)], dst_ref=ref.at[pl.ds(PAD - depth, depth)],
            send_sem=send_sem.at[e, 0], recv_sem=recv_sem.at[e, 0],
            device_id=(tm, sp + 1), device_id_type=MESH)

    def sink(e, ref, depth):
        return pltpu.make_async_remote_copy(
            src_ref=ref.at[pl.ds(PAD, depth)], dst_ref=ref.at[pl.ds(PAD + planes, depth)],
            send_sem=send_sem.at[e, 1], recv_sem=recv_sem.at[e, 1],
            device_id=(tm, sp - 1), device_id_type=MESH)

    posted = {}

    def post(e, ref, depth):
        posted[e] = (ref, depth)
        none = jnp.zeros((depth,) + ref.shape[1:], jnp.float32)

        @pl.when(upper)
        def _():
            rise(e, ref, depth).start()

        @pl.when(jnp.logical_not(upper))
        def _():
            ref[PAD + planes:PAD + planes + depth] = none

        @pl.when(lower)
        def _():
            sink(e, ref, depth).start()

        @pl.when(jnp.logical_not(lower))
        def _():
            ref[PAD - depth:PAD] = none

    def arrive(e):
        ref, depth = posted[e]

        @pl.when(lower)
        def _():
            rise(e, ref, depth).wait_recv()

        @pl.when(upper)
        def _():
            sink(e, ref, depth).wait_recv()

    at_dest = [1.0 - d.astype(jnp.float32) for d in dirs]
    at_src = [d.astype(jnp.float32) for d in dirs]
    hx, hy = 0.5 * drift_x, 0.5 * drift_y

    def advance(role, u, outs, reach=0):
        d = dirs[role]
        dx, dy = at_dest[role] * hx, at_dest[role] * hy
        sx, sy = at_src[role] * hx, at_src[role] * hy
        rows, cols = u.shape[1:]
        for z in range(PAD - reach, PAD + planes + reach):
            v, a = u[z], own[0, d, z]
            w = own[1, d, z] * v
            under = own[1, d, z - 1] * u[z - 1]
            over = own[1, d, z + 1] * u[z + 1]
            vx, vy = sx * v, sy * v
            total = a * (under + over - 6.0 * w)
            total += (a - dx) * pltpu.roll(w + vx, cols - 1, 1)
            total += (a + dx) * pltpu.roll(w - vx, 1, 1)
            total += (a - dy) * pltpu.roll(w + vy, rows - 1, 0)
            total += (a + dy) * pltpu.roll(w - vy, 1, 0)
            for level, extra, dst in outs:
                value = v + tau_levels[level] * total
                dst[z] = value if extra is None else value + extra[z]

    def emit(direction, j):
        if direction == 0:
            dst = forward_out.at[j]
        else:
            dst = adjoint_out.at[steps - 1 - j]
        return pltpu.make_async_copy(points.at[direction, j, mine], dst, out_sem.at[direction, j])

    def finish(role, j):
        @pl.when(dirs[role] == 0)
        def _():
            emit(0, j).start()

        @pl.when(dirs[role] == 1)
        def _():
            emit(1, j).start()

    def hand(slot, src, distance):
        return pltpu.make_async_remote_copy(
            src_ref=src.at[mine], dst_ref=passed.at[slot, mine],
            send_sem=pass_send.at[slot], recv_sem=pass_recv.at[slot],
            device_id=(tm + distance, sp), device_id_type=MESH)

    def forcing(role, j):
        return rhs.at[dirs[role], j]

    def point(role, j):
        return points.at[dirs[role], j]

    m1, m2, t_a1, t_a2, e_tail = [stage.at[i] for i in range(5)]
    e_head = passed.at[E_HEAD]
    first_h, first_t = g_h == 0, g_t == 0
    coarse = powers.at[0]

    def load(direction, j):
        fetch(direction, j).wait()
        if direction == 0:
            for z in range(planes):
                rhs[0, j, PAD + z] += push[j // 4, z]

    chains = [(HEAD, 0), (HEAD, 1), (TAIL, 0), (TAIL, 1)]
    for b in range(2):
        load(0, 4 * b)
        load(1, 4 * b)
    pl.semaphore_wait(barrier, count)
    post(KAPPA, diffuse, 2)
    for role, b in chains:
        post(fine_id(role, b, 0), forcing(role, 4 * b), 1)
    for i in range(1, 4):
        for b in range(2):
            load(0, 4 * b + i)
            load(1, 4 * b + i)
    arrive(KAPPA)
    own[0, 0] = diffuse[...]
    for i in range(3):
        for role, b in chains:
            e = fine_id(role, b, i)
            u = forcing(role, 4 * b) if i == 0 else march.at[role, b, i - 1]
            dst = resid.at[role, b] if i == 2 else march.at[role, b, i]
            arrive(e)
            advance(role, u, [(0, forcing(role, 4 * b + i + 1), dst)])
            if i < 2:
                post(e + 1, dst, 1)
            elif b == 0:
                post(H_R1 if role == HEAD else T_R3, dst, 1)
    h_r1, h_r2, t_r3, t_r4 = resid.at[HEAD, 0], resid.at[HEAD, 1], resid.at[TAIL, 0], resid.at[TAIL, 1]
    t_m1, t_r1, t_r2 = passed.at[M1], passed.at[R1], passed.at[R2]
    partner = sign_h
    arrive(H_R1)
    advance(HEAD, h_r1, [(1, h_r2, m1)])
    hand(M1, m1, partner).start()
    for role in (HEAD, TAIL):
        post(FIFTH + role, forcing(role, 5), 1)
    arrive(T_R3)
    hand(M1, m1, partner).wait_recv()
    post(T_M1, t_m1, 2)
    hand(R1, h_r1, partner).start()
    hand(R2, h_r2, partner).start()
    arrive(T_M1)
    advance(TAIL, t_m1, [(1, t_r3, m2)], 1)
    advance(TAIL, m2, [(1, t_r4, coarse)])

    h_a1, h_a2, t_a3, t_e = point(HEAD, 3), point(HEAD, 7), point(TAIL, 3), point(TAIL, 7)

    def part(i):
        return pltpu.make_async_remote_copy(
            src_ref=powers.at[i, mine], dst_ref=parts.at[i],
            send_sem=part_send.at[i], recv_sem=part_recv.at[i],
            device_id=(tm + sign_t * (2 * i + 2), sp), device_id_type=MESH)

    for i in range(groups - 1):
        @pl.when(g_t + 1 + i < groups)
        def _():
            if i % 2 == 1:
                e = POWERS + i // 2
                post(e, powers.at[i - 1], 2)
                arrive(e)
                advance(TAIL, powers.at[i - 1], [(2, None, powers.at[i])], 1)
            elif i > 0:
                advance(TAIL, powers.at[i - 1], [(2, None, powers.at[i])])
            part(i).start()

    hand(R1, h_r1, partner).wait_recv()
    post(T_R1, t_r1, 1)

    def tail0():
        e_tail[mid] = jnp.zeros((planes,) + e_tail.shape[1:], jnp.float32)
        for i in range(groups - 1):
            @pl.when(i < g_t)
            def _():
                part(i).wait_recv()
                for z in range(planes):
                    e_tail[PAD + z] += parts[i, z]

        post(T_E, e_tail, 2)

        @pl.when(jnp.logical_not(first_t))
        def _():
            hand(E_HEAD, e_tail, partner).start()

    def tail1():
        arrive(T_R1)
        hand(R2, h_r2, partner).wait_recv()
        arrive(T_E)
        advance(TAIL, e_tail, [(1, t_r1, t_a1)], 1)
        advance(TAIL, t_a1, [(1, t_r2, t_a2)])
        post(T_A2, t_a2, 2)
        advance(TAIL, e_tail, [(2, coarse, t_e)])
        finish(TAIL, 7)

    def tail2():
        arrive(FIFTH + TAIL)
        arrive(T_A2)
        advance(TAIL, t_a2, [(1, t_r3, t_a3), (0, forcing(TAIL, 0), point(TAIL, 0))], 1)
        advance(TAIL, t_a3, [(0, forcing(TAIL, 4), point(TAIL, 4))])
        post(LATE + TAIL * 2, point(TAIL, 4), 2)
        advance(TAIL, point(TAIL, 0), [(0, forcing(TAIL, 1), point(TAIL, 1))])
        post(LATE + TAIL * 2 + 1, point(TAIL, 1), 1)
        for j in (3, 0, 4, 1):
            finish(TAIL, j)

    def last(role):
        arrive(LATE + role * 2)
        advance(role, point(role, 4), [(0, forcing(role, 5), point(role, 5))], 1)
        advance(role, point(role, 5), [(0, forcing(role, 6), point(role, 6))])
        finish(role, 5)
        finish(role, 6)
        arrive(LATE + role * 2 + 1)
        advance(role, point(role, 1), [(0, forcing(role, 2), point(role, 2))])
        finish(role, 2)

    def tail3():
        last(TAIL)

    def head0():
        @pl.when(first_h)
        def _():
            e_head[mid] = jnp.zeros((planes,) + e_head.shape[1:], jnp.float32)

        @pl.when(jnp.logical_not(first_h))
        def _():
            hand(E_HEAD, e_tail, partner).wait_recv()

        post(H_E, e_head, 2)

    def head1():
        arrive(FIFTH + HEAD)
        arrive(H_E)
        advance(HEAD, e_head, [(1, h_r1, h_a1), (0, forcing(HEAD, 0), point(HEAD, 0))], 1)
        advance(HEAD, h_a1, [(0, forcing(HEAD, 4), point(HEAD, 4)), (1, h_r2, h_a2)])
        post(LATE + HEAD * 2, point(HEAD, 4), 2)
        advance(HEAD, point(HEAD, 0), [(0, forcing(HEAD, 1), point(HEAD, 1))])
        post(LATE + HEAD * 2 + 1, point(HEAD, 1), 1)
        for j in (3, 0, 4, 7, 1):
            finish(HEAD, j)

    def head2():
        last(HEAD)

    @pl.when(first_h)
    def _():
        for piece in (head0, head1, tail0, tail1, head2, tail2, tail3):
            piece()

    @pl.when(jnp.logical_not(first_h))
    def _():
        for piece in (tail0, tail1, head0, tail2, head1, tail3, head2):
            piece()

    def settle(e, ref, depth):

        @pl.when(upper)
        def _():
            rise(e, ref, depth).wait_send()

        @pl.when(lower)
        def _():
            sink(e, ref, depth).wait_send()

    for e in range(LATE):
        settle(e, *posted[e])
    for role in (HEAD, TAIL):
        settle(LATE + role * 2, point(role, 4), 2)
        settle(LATE + role * 2 + 1, point(role, 1), 1)
    hand(M1, m1, partner).wait_send()
    hand(R1, h_r1, partner).wait_send()
    hand(R2, h_r2, partner).wait_send()

    @pl.when(jnp.logical_not(first_t))
    def _():
        hand(E_HEAD, e_tail, partner).wait_send()


    for i in range(groups - 1):
        @pl.when(g_t + 1 + i < groups)
        def _():
            part(i).wait_send()
            if i % 2 == 1:
                settle(POWERS + i // 2, powers.at[i - 1], 2)
    for j in range(steps):
        emit(0, j).wait()
        emit(1, j).wait()


def solution(mesh):
    members, slabs = mesh.shape["tm"], mesh.shape["space"]

    def on_device(source, thrust_axial, thrust_lateral, yaw_index, diffusivity, cotangent):
        steps = source.shape[0]
        links = members // 2 - 1
        exchanges = POWERS + max(1, links // 2)
        slab = diffusivity.shape
        wide = (slab[0] + 2 * PAD,) + slab[1:]
        anywhere = pl.BlockSpec(memory_space=pl.ANY)
        f32 = jnp.float32
        return pl.pallas_call(
            functools.partial(kernel, members, slabs),
            out_shape=(jax.ShapeDtypeStruct(source.shape, f32), jax.ShapeDtypeStruct(source.shape, f32)),
            in_specs=[anywhere] * 6,
            out_specs=(anywhere, anywhere),
            scratch_shapes=[
                pltpu.SMEM(yaw_index.shape, jnp.int32),
                pltpu.VMEM(slab, f32),
                pltpu.VMEM(slab, f32),
                pltpu.VMEM(slab, f32),
                pltpu.VMEM((2, steps) + wide, f32),
                pltpu.VMEM((2, steps) + wide, f32),
                pltpu.VMEM((2, 2) + wide, f32),
                pltpu.VMEM((2,) + slab, f32),
                pltpu.VMEM((2, 2, 2) + wide, f32),
                pltpu.VMEM((2, 2) + wide, f32),
                pltpu.VMEM((5,) + wide, f32),
                pltpu.VMEM((4,) + wide, f32),
                pltpu.VMEM((links,) + wide, f32),
                pltpu.VMEM((links,) + slab, f32),
                pltpu.SemaphoreType.DMA((exchanges, 2)),
                pltpu.SemaphoreType.DMA((exchanges, 2)),
                pltpu.SemaphoreType.DMA((4,)),
                pltpu.SemaphoreType.DMA((4,)),
                pltpu.SemaphoreType.DMA((links,)),
                pltpu.SemaphoreType.DMA((links,)),
                pltpu.SemaphoreType.DMA((2, steps)),
                pltpu.SemaphoreType.DMA((2, steps)),
                pltpu.SemaphoreType.DMA((4,)),
            ],
            compiler_params=pltpu.CompilerParams(
                collective_id=0, has_side_effects=True, vmem_limit_bytes=60 * 1024 * 1024),
            cost_estimate=pl.CostEstimate(flops=40_000_000, bytes_accessed=4_500_000, transcendentals=0),
        )(yaw_index, thrust_axial, thrust_lateral, diffusivity, source, cotangent)

    return jax.shard_map(
        on_device,
        mesh=mesh,
        in_specs=(
            P("tm", "space", None, None),
            P("space", None, None),
            P("space", None, None),
            P("tm"),
            P("space", None, None),
            P("tm", "space", None, None),
        ),
        out_specs=(P("tm", "space", None, None), P("tm", "space", None, None)),
        check_vma=False,
    )
```

```python
import functools
import math

import jax
import jax.numpy as jnp
from jax import lax
from jax.experimental import pallas as pl
from jax.experimental.pallas import tpu as pltpu
from jax.sharding import PartitionSpec as P

YAWS = 24
MESH = pl.DeviceIdType.MESH

tau_levels = (0.03, 0.06, 0.08)
drift_x = 0.3
drift_y = 0.2

HEAD, TAIL = 0, 1
KAPPA, H_R1, T_R3, T_R1, T_M1, T_E, H_E, T_A2 = range(12, 20)
FIFTH, LATE, POWERS = 20, 22, 26
PAD = 2
M1, R1, R2, E_HEAD = 0, 1, 2, 3


def fine_id(role, block, step):
    return (role * 2 + block) * 3 + step


def kernel(
    members, slabs,
    yaw_hbm, axial_hbm, lateral_hbm, kappa_hbm, source, cotangent,
    forward_out, adjoint_out,
    yaw, axial, lateral, kappa, rhs, points, own, push, march, resid, stage, passed, powers, parts,
    send_sem, recv_sem, pass_send, pass_recv, part_send, part_recv, in_sem, out_sem, small_sem,
):
    planes = kappa.shape[0]
    steps = source.shape[0]
    groups = members // 2
    mid = slice(PAD, PAD + planes)
    mine = pl.ds(PAD, planes)
    tm, sp = lax.axis_index("tm"), lax.axis_index("space")
    dir_h = lax.rem(tm, 2)
    dir_t = 1 - dir_h
    sign_h = 1 - 2 * dir_h
    sign_t = -sign_h
    pos_h = jnp.where(dir_h == 0, tm, members - 1 - tm)
    g_h = pos_h // 2
    g_t = groups - 1 - g_h
    dirs = (dir_h, dir_t)
    lower, upper = sp > 0, sp < slabs - 1
    neighbours = [(lower, tm, sp - 1), (upper, tm, sp + 1)]
    for t in range(members):
        alike = jnp.logical_and(lax.rem(tm + t, 2) == 0, tm != t)
        neighbours.append((jnp.logical_or(alike, tm + sign_h == t), t, sp))
    barrier = pltpu.get_barrier_semaphore()
    count = 0
    for there, t, s in neighbours:
        count = count + there.astype(jnp.int32)

        @pl.when(there)
        def _():
            pl.semaphore_signal(barrier, inc=1, device_id=(t, s), device_id_type=MESH)

    def fetch(direction, j):
        if direction == 0:
            src = source.at[j]
        else:
            src = cotangent.at[steps - 1 - j]
        return pltpu.make_async_copy(src, rhs.at[direction, j, mine], in_sem.at[direction, j])

    small = [
        pltpu.make_async_copy(src, dst, small_sem.at[i])
        for i, (src, dst) in enumerate(
            ((yaw_hbm, yaw), (kappa_hbm, kappa), (axial_hbm, axial), (lateral_hbm, lateral)))
    ]
    for copy in small:
        copy.start()
    for i in range(4):
        for b in range(2):
            fetch(0, 4 * b + i).start()
            fetch(1, 4 * b + i).start()

    def rise(e, ref, depth):
        return pltpu.make_async_remote_copy(
            src_ref=ref.at[pl.ds(PAD + planes - depth, depth)], dst_ref=ref.at[pl.ds(PAD - depth, depth)],
            send_sem=send_sem.at[e, 0], recv_sem=recv_sem.at[e, 0],
            device_id=(tm, sp + 1), device_id_type=MESH)

    def sink(e, ref, depth):
        return pltpu.make_async_remote_copy(
            src_ref=ref.at[pl.ds(PAD, depth)], dst_ref=ref.at[pl.ds(PAD + planes, depth)],
            send_sem=send_sem.at[e, 1], recv_sem=recv_sem.at[e, 1],
            device_id=(tm, sp - 1), device_id_type=MESH)

    posted = {}

    def post(e, ref, depth):
        posted[e] = (ref, depth)
        none = jnp.zeros((depth,) + ref.shape[1:], jnp.float32)

        @pl.when(upper)
        def _():
            rise(e, ref, depth).start()

        @pl.when(jnp.logical_not(upper))
        def _():
            ref[PAD + planes:PAD + planes + depth] = none

        @pl.when(lower)
        def _():
            sink(e, ref, depth).start()

        @pl.when(jnp.logical_not(lower))
        def _():
            ref[PAD - depth:PAD] = none

    def arrive(e):
        ref, depth = posted[e]

        @pl.when(lower)
        def _():
            rise(e, ref, depth).wait_recv()

        @pl.when(upper)
        def _():
            sink(e, ref, depth).wait_recv()

    at_dest = [1.0 - d.astype(jnp.float32) for d in dirs]
    at_src = [d.astype(jnp.float32) for d in dirs]
    hx, hy = 0.5 * drift_x, 0.5 * drift_y

    def advance(role, u, outs, reach=0):
        d = dirs[role]
        dx, dy = at_dest[role] * hx, at_dest[role] * hy
        sx, sy = at_src[role] * hx, at_src[role] * hy
        rows, cols = u.shape[1:]
        for z in range(PAD - reach, PAD + planes + reach):
            v, a = u[z], own[0, d, z]
            w = own[1, d, z] * v
            under = own[1, d, z - 1] * u[z - 1]
            over = own[1, d, z + 1] * u[z + 1]
            vx, vy = sx * v, sy * v
            total = a * (under + over - 6.0 * w)
            total += (a - dx) * pltpu.roll(w + vx, cols - 1, 1)
            total += (a + dx) * pltpu.roll(w - vx, 1, 1)
            total += (a - dy) * pltpu.roll(w + vy, rows - 1, 0)
            total += (a + dy) * pltpu.roll(w - vy, 1, 0)
            for level, extra, dst in outs:
                value = v + tau_levels[level] * total
                dst[z] = value if extra is None else value + extra[z]

    def emit(direction, j):
        if direction == 0:
            dst = forward_out.at[j]
        else:
            dst = adjoint_out.at[steps - 1 - j]
        return pltpu.make_async_copy(points.at[direction, j, mine], dst, out_sem.at[direction, j])

    def finish(role, j):
        @pl.when(dirs[role] == 0)
        def _():
            emit(0, j).start()

        @pl.when(dirs[role] == 1)
        def _():
            emit(1, j).start()

    def hand(slot, src, distance):
        return pltpu.make_async_remote_copy(
            src_ref=src.at[mine], dst_ref=passed.at[slot, mine],
            send_sem=pass_send.at[slot], recv_sem=pass_recv.at[slot],
            device_id=(tm + distance, sp), device_id_type=MESH)

    def forcing(role, j):
        return rhs.at[dirs[role], j]

    def point(role, j):
        return points.at[dirs[role], j]

    m1, m2, t_a1, t_a2, e_tail = [stage.at[i] for i in range(5)]
    e_head = passed.at[E_HEAD]
    first_h, first_t = g_h == 0, g_t == 0
    coarse = powers.at[0]

    def load(direction, j):
        fetch(direction, j).wait()
        if direction == 0:
            for z in range(planes):
                rhs[0, j, PAD + z] += push[j // 4, z]

    chains = [(HEAD, 0), (HEAD, 1), (TAIL, 0), (TAIL, 1)]
    small[1].wait()
    wide = own.shape[2:]
    own[0, 1] = jnp.ones(wide, jnp.float32)
    own[1, 0] = jnp.ones(wide, jnp.float32)
    diffuse = own.at[1, 1]
    diffuse[mid] = kappa[...]
    pl.semaphore_wait(barrier, count)
    post(KAPPA, diffuse, 2)
    for i in (0, 2, 3):
        small[i].wait()
    for b in range(2):
        angle = (2.0 * math.pi / YAWS) * jnp.full(kappa.shape[1:], yaw[b], jnp.int32).astype(jnp.float32)
        c, s = jnp.cos(angle[:8]), jnp.sin(angle[:8])
        reps = kappa.shape[1] // 8
        c, s = jnp.concatenate([c] * reps, 0), jnp.concatenate([s] * reps, 0)
        for z in range(planes):
            push[b, z] = c * axial[z] + s * lateral[z]

    for b in range(2):
        load(0, 4 * b)
        load(1, 4 * b)
    for role, b in chains:
        post(fine_id(role, b, 0), forcing(role, 4 * b), 1)
    for i in range(1, 4):
        for b in range(2):
            load(0, 4 * b + i)
            load(1, 4 * b + i)
    arrive(KAPPA)
    own[0, 0] = diffuse[...]
    for i in range(3):
        for role, b in chains:
            e = fine_id(role, b, i)
            u = forcing(role, 4 * b) if i == 0 else march.at[role, b, i - 1]
            dst = resid.at[role, b] if i == 2 else march.at[role, b, i]
            arrive(e)
            advance(role, u, [(0, forcing(role, 4 * b + i + 1), dst)])
            if i < 2:
                post(e + 1, dst, 1)
            elif b == 0:
                post(H_R1 if role == HEAD else T_R3, dst, 1)
    h_r1, h_r2, t_r3, t_r4 = resid.at[HEAD, 0], resid.at[HEAD, 1], resid.at[TAIL, 0], resid.at[TAIL, 1]
    t_m1, t_r1, t_r2 = passed.at[M1], passed.at[R1], passed.at[R2]
    partner = sign_h
    arrive(H_R1)
    advance(HEAD, h_r1, [(1, h_r2, m1)])
    hand(M1, m1, partner).start()
    for role in (HEAD, TAIL):
        post(FIFTH + role, forcing(role, 5), 1)
    arrive(T_R3)
    hand(M1, m1, partner).wait_recv()
    post(T_M1, t_m1, 2)
    hand(R1, h_r1, partner).start()
    hand(R2, h_r2, partner).start()
    arrive(T_M1)
    advance(TAIL, t_m1, [(1, t_r3, m2)], 1)
    advance(TAIL, m2, [(1, t_r4, coarse)])

    h_a1, h_a2, t_a3, t_e = point(HEAD, 3), point(HEAD, 7), point(TAIL, 3), point(TAIL, 7)

    def part(i):
        return pltpu.make_async_remote_copy(
            src_ref=powers.at[i, mine], dst_ref=parts.at[i],
            send_sem=part_send.at[i], recv_sem=part_recv.at[i],
            device_id=(tm + sign_t * (2 * i + 2), sp), device_id_type=MESH)

    for i in range(groups - 1):
        @pl.when(g_t + 1 + i < groups)
        def _():
            if i % 2 == 1:
                e = POWERS + i // 2
                post(e, powers.at[i - 1], 2)
                arrive(e)
                advance(TAIL, powers.at[i - 1], [(2, None, powers.at[i])], 1)
            elif i > 0:
                advance(TAIL, powers.at[i - 1], [(2, None, powers.at[i])])
            part(i).start()

    hand(R1, h_r1, partner).wait_recv()
    post(T_R1, t_r1, 1)

    def tail0():
        e_tail[mid] = jnp.zeros((planes,) + e_tail.shape[1:], jnp.float32)
        for i in range(groups - 1):
            @pl.when(i < g_t)
            def _():
                part(i).wait_recv()
                for z in range(planes):
                    e_tail[PAD + z] += parts[i, z]

        post(T_E, e_tail, 2)

        @pl.when(jnp.logical_not(first_t))
        def _():
            hand(E_HEAD, e_tail, partner).start()

    def tail1():
        arrive(T_R1)
        hand(R2, h_r2, partner).wait_recv()
        arrive(T_E)
        advance(TAIL, e_tail, [(1, t_r1, t_a1)], 1)
        advance(TAIL, t_a1, [(1, t_r2, t_a2)])
        post(T_A2, t_a2, 2)
        advance(TAIL, e_tail, [(2, coarse, t_e)])
        finish(TAIL, 7)

    def tail2():
        arrive(FIFTH + TAIL)
        arrive(T_A2)
        advance(TAIL, t_a2, [(1, t_r3, t_a3), (0, forcing(TAIL, 0), point(TAIL, 0))], 1)
        advance(TAIL, t_a3, [(0, forcing(TAIL, 4), point(TAIL, 4))])
        post(LATE + TAIL * 2, point(TAIL, 4), 2)
        advance(TAIL, point(TAIL, 0), [(0, forcing(TAIL, 1), point(TAIL, 1))])
        post(LATE + TAIL * 2 + 1, point(TAIL, 1), 1)
        for j in (3, 0, 4, 1):
            finish(TAIL, j)

    def last(role):
        arrive(LATE + role * 2)
        advance(role, point(role, 4), [(0, forcing(role, 5), point(role, 5))], 1)
        advance(role, point(role, 5), [(0, forcing(role, 6), point(role, 6))])
        finish(role, 5)
        finish(role, 6)
        arrive(LATE + role * 2 + 1)
        advance(role, point(role, 1), [(0, forcing(role, 2), point(role, 2))])
        finish(role, 2)

    def tail3():
        last(TAIL)

    def head0():
        @pl.when(first_h)
        def _():
            e_head[mid] = jnp.zeros((planes,) + e_head.shape[1:], jnp.float32)

        @pl.when(jnp.logical_not(first_h))
        def _():
            hand(E_HEAD, e_tail, partner).wait_recv()

        post(H_E, e_head, 2)

    def head1():
        arrive(FIFTH + HEAD)
        arrive(H_E)
        advance(HEAD, e_head, [(1, h_r1, h_a1), (0, forcing(HEAD, 0), point(HEAD, 0))], 1)
        advance(HEAD, h_a1, [(0, forcing(HEAD, 4), point(HEAD, 4)), (1, h_r2, h_a2)])
        post(LATE + HEAD * 2, point(HEAD, 4), 2)
        advance(HEAD, point(HEAD, 0), [(0, forcing(HEAD, 1), point(HEAD, 1))])
        post(LATE + HEAD * 2 + 1, point(HEAD, 1), 1)
        for j in (3, 0, 4, 7, 1):
            finish(HEAD, j)

    def head2():
        last(HEAD)

    @pl.when(first_h)
    def _():
        for piece in (head0, head1, tail0, tail1, head2, tail2, tail3):
            piece()

    @pl.when(jnp.logical_not(first_h))
    def _():
        for piece in (tail0, tail1, head0, tail2, head1, tail3, head2):
            piece()

    def settle(e, ref, depth):

        @pl.when(upper)
        def _():
            rise(e, ref, depth).wait_send()

        @pl.when(lower)
        def _():
            sink(e, ref, depth).wait_send()

    for e in range(LATE):
        settle(e, *posted[e])
    for role in (HEAD, TAIL):
        settle(LATE + role * 2, point(role, 4), 2)
        settle(LATE + role * 2 + 1, point(role, 1), 1)
    hand(M1, m1, partner).wait_send()
    hand(R1, h_r1, partner).wait_send()
    hand(R2, h_r2, partner).wait_send()

    @pl.when(jnp.logical_not(first_t))
    def _():
        hand(E_HEAD, e_tail, partner).wait_send()


    for i in range(groups - 1):
        @pl.when(g_t + 1 + i < groups)
        def _():
            part(i).wait_send()
            if i % 2 == 1:
                settle(POWERS + i // 2, powers.at[i - 1], 2)
    for j in range(steps):
        emit(0, j).wait()
        emit(1, j).wait()


def solution(mesh):
    members, slabs = mesh.shape["tm"], mesh.shape["space"]

    def on_device(source, thrust_axial, thrust_lateral, yaw_index, diffusivity, cotangent):
        steps = source.shape[0]
        links = members // 2 - 1
        exchanges = POWERS + max(1, links // 2)
        slab = diffusivity.shape
        wide = (slab[0] + 2 * PAD,) + slab[1:]
        anywhere = pl.BlockSpec(memory_space=pl.ANY)
        f32 = jnp.float32
        return pl.pallas_call(
            functools.partial(kernel, members, slabs),
            out_shape=(jax.ShapeDtypeStruct(source.shape, f32), jax.ShapeDtypeStruct(source.shape, f32)),
            in_specs=[anywhere] * 6,
            out_specs=(anywhere, anywhere),
            scratch_shapes=[
                pltpu.SMEM(yaw_index.shape, jnp.int32),
                pltpu.VMEM(slab, f32),
                pltpu.VMEM(slab, f32),
                pltpu.VMEM(slab, f32),
                pltpu.VMEM((2, steps) + wide, f32),
                pltpu.VMEM((2, steps) + wide, f32),
                pltpu.VMEM((2, 2) + wide, f32),
                pltpu.VMEM((2,) + slab, f32),
                pltpu.VMEM((2, 2, 2) + wide, f32),
                pltpu.VMEM((2, 2) + wide, f32),
                pltpu.VMEM((5,) + wide, f32),
                pltpu.VMEM((4,) + wide, f32),
                pltpu.VMEM((links,) + wide, f32),
                pltpu.VMEM((links,) + slab, f32),
                pltpu.SemaphoreType.DMA((exchanges, 2)),
                pltpu.SemaphoreType.DMA((exchanges, 2)),
                pltpu.SemaphoreType.DMA((4,)),
                pltpu.SemaphoreType.DMA((4,)),
                pltpu.SemaphoreType.DMA((links,)),
                pltpu.SemaphoreType.DMA((links,)),
                pltpu.SemaphoreType.DMA((2, steps)),
                pltpu.SemaphoreType.DMA((2, steps)),
                pltpu.SemaphoreType.DMA((4,)),
            ],
            compiler_params=pltpu.CompilerParams(
                collective_id=0, has_side_effects=True, vmem_limit_bytes=60 * 1024 * 1024),
            cost_estimate=pl.CostEstimate(flops=40_000_000, bytes_accessed=4_500_000, transcendentals=0),
        )(yaw_index, thrust_axial, thrust_lateral, diffusivity, source, cotangent)

    return jax.shard_map(
        on_device,
        mesh=mesh,
        in_specs=(
            P("tm", "space", None, None),
            P("space", None, None),
            P("space", None, None),
            P("tm"),
            P("space", None, None),
            P("tm", "space", None, None),
        ),
        out_specs=(P("tm", "space", None, None), P("tm", "space", None, None)),
        check_vma=False,
    )
```
